32 devices in a mesh: dp: 8 (over y, x, core), mp: 4 (over z).
Axes of the slice: x: 2, y: 2, z: 4, core: 2. Of those that a mesh axis runs over, the one named last changes fastest.
Arguments:
- block_input: bfloat16 [8192, 2048], P(('dp', 'mp')), may hold values from -6 to 6
- cotangent: bfloat16 [8192, 2048], P(('dp', 'mp')), may hold values from -6 to 6
- lengths: int32 [8], replicated, may hold values from 256 to 1024, as said below
- vectors: float32 [4, 2048], replicated, may hold values from 0.5 to 1.5, as said below
- vectors_first: float32 [4, 2048], replicated, may hold values from -60 to 60
- vectors_second: float32 [4, 2048], replicated, may hold values from 1 to 1000
- mixer_in: float32 [3, 2048, 2048], P(None, 'dp', 'mp'), may hold values from -0.125 to 0.125
- mixer_in_first: float32 [3, 2048, 2048], P(None, 'dp', 'mp'), may hold values from -60 to 60
- mixer_in_second: float32 [3, 2048, 2048], P(None, 'dp', 'mp'), may hold values from 1 to 1000
- mixer_out: float32 [2048, 2048], P('mp', 'dp'), may hold values from -0.125 to 0.125
- mixer_out_first: float32 [2048, 2048], P('mp', 'dp'), may hold values from -60 to 60
- mixer_out_second: float32 [2048, 2048], P('mp', 'dp'), may hold values from 1 to 1000
- ffn_in: float32 [2, 2048, 5632], P(None, 'dp', 'mp'), may hold values from -0.125 to 0.125
- ffn_in_first: float32 [2, 2048, 5632], P(None, 'dp', 'mp'), may hold values from -60 to 60
- ffn_in_second: float32 [2, 2048, 5632], P(None, 'dp', 'mp'), may hold values from 1 to 1000
- ffn_out: float32 [5632, 2048], P('mp', 'dp'), may hold values from -0.078125 to 0.078125
- ffn_out_first: float32 [5632, 2048], P('mp', 'dp'), may hold values from -60 to 60
- ffn_out_second: float32 [5632, 2048], P('mp', 'dp'), may hold values from 1 to 1000
Outputs:
- block_output: bfloat16 [8192, 2048], P(('dp', 'mp'))
- input_grad: float32 [8192, 2048], P(('dp', 'mp'))
- stats: float32 [3], replicated
- vectors_grad: float32 [4, 2048], replicated
- vectors_first_new: float32 [4, 2048], replicated
- vectors_second_new: float32 [4, 2048], replicated
- mixer_in_grad: float32 [3, 2048, 2048], P(None, 'dp', 'mp')
- mixer_in_new: float32 [3, 2048, 2048], P(None, 'dp', 'mp')
- mixer_in_first_new: float32 [3, 2048, 2048], P(None, 'dp', 'mp')
- mixer_in_second_new: float32 [3, 2048, 2048], P(None, 'dp', 'mp')
- mixer_in_bf16: bfloat16 [3, 2048, 2048], P(None, None, 'mp')
- mixer_out_grad: float32 [2048, 2048], P('mp', 'dp')
- mixer_out_new: float32 [2048, 2048], P('mp', 'dp')
- mixer_out_first_new: float32 [2048, 2048], P('mp', 'dp')
- mixer_out_second_new: float32 [2048, 2048], P('mp', 'dp')
- mixer_out_bf16: bfloat16 [2048, 2048], P('mp')
- ffn_in_grad: float32 [2, 2048, 5632], P(None, 'dp', 'mp')
- ffn_in_new: float32 [2, 2048, 5632], P(None, 'dp', 'mp')
- ffn_in_first_new: float32 [2, 2048, 5632], P(None, 'dp', 'mp')
- ffn_in_second_new: float32 [2, 2048, 5632], P(None, 'dp', 'mp')
- ffn_in_bf16: bfloat16 [2, 2048, 5632], P(None, None, 'mp')
- ffn_out_grad: float32 [5632, 2048], P('mp', 'dp')
- ffn_out_new: float32 [5632, 2048], P('mp', 'dp')
- ffn_out_first_new: float32 [5632, 2048], P('mp', 'dp')
- ffn_out_second_new: float32 [5632, 2048], P('mp', 'dp')
- ffn_out_bf16: bfloat16 [5632, 2048], P('mp')
The draws below stay inside these ranges and needn't reach their ends.
Inputs may be any that keep to these rules, and one draw needn't show every extreme that they name: `lengths`: each sequence's valid slots come first; sequence 0 is full (1024 valid slots). `vectors`: rows 0, 1 and 3 are gains; row 2 lies in 0.85 to 0.97.
All inputs are finite; a program needn't handle non-finite values.
Results may differ from the reference program's by a relative error of at most 0.02.
Values may be sent and summed in bfloat16 or wider, within the bound.
No kernel may reach another device: no remote copies, remote signals or barrier semaphores. Data moves between devices by JAX's collectives and lax.ppermute only.
A program may use at most 320 MiB of HBM per device.

```python
import math
import jax
import jax.numpy as jnp
from jax import lax

D = 2048
HEAD = 128
FF = 5632
SLOTS = 1024
MINLEN = 256
SPAN = 64
STEP = 10
SEQS = 8
TOKENS = 8192


def draw_lengths(key, part):
    drawn = jax.random.randint(key, (SEQS,), MINLEN, SLOTS + 1)
    return drawn.at[0].set(SLOTS)


def draw_vectors(key, part):
    gain_key = jax.random.fold_in(key, 11)
    bound_key = jax.random.fold_in(key, 23)
    gains = 1.0 + 0.12 * jax.random.normal(gain_key, (3, D), jnp.float32)
    gains = jnp.clip(gains, 0.5, 1.5)
    lower = jax.random.uniform(bound_key, (D,), jnp.float32, 0.85, 0.97)
    return jnp.stack([gains[0], gains[1], lower, gains[2]])


def levels(own_key, extent, cuts, low, largest):
    level = 1.0
    for dim, shards_of in cuts:
        heights = jax.random.uniform(jax.random.fold_in(jax.random.fold_in(own_key, 6), dim), (shards_of,), jnp.float32, low / len(cuts), largest / len(cuts))
        level = level * jnp.repeat(jnp.exp(heights), extent[dim] // shards_of).reshape((-1,) + (1,) * (len(extent) - 1 - dim))
    return level


def bell_draw(rng, shape, spread, reach, cuts=(), kind=jnp.bfloat16):
    entries = spread * jax.random.normal(rng, shape, jnp.float32)
    if cuts:
        entries = entries * levels(rng, shape, cuts, -0.22, 0.18)
    return jnp.clip(entries, -reach, reach).astype(kind)


def setup_inputs(seed: int = 0) -> dict:
    streams_of = jax.random.split(jax.random.key(seed), 19)
    return {
        "block_input": bell_draw(streams_of[0], (TOKENS, D), 1.0, 6.0, ((0, 32),)),
        "cotangent": bell_draw(streams_of[1], (TOKENS, D), 1.0, 6.0, ((0, 32),)),
        "lengths": draw_lengths(jax.random.fold_in(streams_of[18], 71), 0),
        "vectors": draw_vectors(jax.random.fold_in(streams_of[18], 71), 0),
        "vectors_first": bell_draw(streams_of[4], (4, D), 10.0, 60.0, (), jnp.float32),
        "vectors_second": jnp.clip(jnp.exp(jax.random.uniform(streams_of[5], (4, D), jnp.float32, math.log(1.0), math.log(1000.0))), 1.0, 1000.0),
        "mixer_in": bell_draw(streams_of[6], (3, D, D), D ** -0.5, 0.125, ((1, 8), (2, 4)), jnp.float32),
        "mixer_in_first": bell_draw(streams_of[7], (3, D, D), 10.0, 60.0, ((1, 8), (2, 4)), jnp.float32),
        "mixer_in_second": jnp.clip(jnp.exp(math.log(1000.0) - 6.9077553 * jax.random.uniform(streams_of[8], (3, D, D), jnp.float32) ** levels(streams_of[8], (3, D, D), ((1, 8), (2, 4)), -0.2, 0.2)), 1.0, 1000.0),
        "mixer_out": bell_draw(streams_of[9], (D, D), D ** -0.5, 0.125, ((0, 4), (1, 8)), jnp.float32),
        "mixer_out_first": bell_draw(streams_of[10], (D, D), 10.0, 60.0, ((0, 4), (1, 8)), jnp.float32),
        "mixer_out_second": jnp.clip(jnp.exp(math.log(1000.0) - 6.9077553 * jax.random.uniform(streams_of[11], (D, D), jnp.float32) ** levels(streams_of[11], (D, D), ((0, 4), (1, 8)), -0.2, 0.2)), 1.0, 1000.0),
        "ffn_in": bell_draw(streams_of[12], (2, D, FF), D ** -0.5, 0.125, ((1, 8), (2, 4)), jnp.float32),
        "ffn_in_first": bell_draw(streams_of[13], (2, D, FF), 10.0, 60.0, ((1, 8), (2, 4)), jnp.float32),
        "ffn_in_second": jnp.clip(jnp.exp(math.log(1000.0) - 6.9077553 * jax.random.uniform(streams_of[14], (2, D, FF), jnp.float32) ** levels(streams_of[14], (2, D, FF), ((1, 8), (2, 4)), -0.2, 0.2)), 1.0, 1000.0),
        "ffn_out": bell_draw(streams_of[15], (FF, D), FF ** -0.5, 0.078125, ((0, 4), (1, 8)), jnp.float32),
        "ffn_out_first": bell_draw(streams_of[16], (FF, D), 10.0, 60.0, ((0, 4), (1, 8)), jnp.float32),
        "ffn_out_second": jnp.clip(jnp.exp(math.log(1000.0) - 6.9077553 * jax.random.uniform(streams_of[17], (FF, D), jnp.float32) ** levels(streams_of[17], (FF, D), ((0, 4), (1, 8)), -0.2, 0.2)), 1.0, 1000.0),
    }


EPS = 1e-06
BETA_ONE = 0.9
BETA_TWO = 0.95
DECAY = 0.1
ADAM_EPS = 1e-08
LEARN_RATE = 0.005

@jax.custom_vjp
def low(v):
    return lax.optimization_barrier(v.astype(jnp.bfloat16)).astype(jnp.float32)

@jax.custom_vjp
def low_back(v):
    return v

def low_keep(v):
    return (low(v), None)

def low_pass(kept, grad):
    return (grad,)

def back_keep(v):
    return (v, None)

def back_low(kept, grad):
    return (low(grad),)
low.defvjp(low_keep, low_pass)
low_back.defvjp(back_keep, back_low)

def matmul(left, right):
    return jnp.dot(left, right, precision=lax.Precision.HIGHEST, preferred_element_type=jnp.float32)

def rms_norm(value, gain):
    return value * lax.rsqrt(lax.optimization_barrier(jnp.mean(value * value, axis=-1, keepdims=True)) + EPS) * gain

def recurrence(query, log_forget, key, value):
    length, heads, width = query.shape
    blocks = length // SPAN
    shape = (blocks, SPAN, heads, width)
    parts = (query.reshape(shape), log_forget.reshape(shape), key.reshape(shape), value.reshape(shape))
    lower_tri = jnp.arange(SPAN)[:, None] >= jnp.arange(SPAN)[None, :]
    highest_precision = lax.Precision.HIGHEST

    def block(running_state, piece):
        query_block, decay_block, key_block, value_block_rows = piece
        running = jnp.cumsum(decay_block, axis=0)
        final_state = running[-1]
        decayed_query_rows = query_block * jnp.exp(running)
        key_decayed = key_block * jnp.exp(-running)
        inter_block_output = jnp.einsum('xil,ilf->xif', decayed_query_rows, running_state, precision=highest_precision)
        scores = jnp.einsum('chk,shk->hcs', decayed_query_rows, key_decayed, precision=highest_precision)
        scores = jnp.where(lower_tri[None], scores, 0.0)
        intra = jnp.einsum('hcs,shv->chv', scores, value_block_rows, precision=highest_precision)
        carried_state = key_block * jnp.exp(final_state[None] - running)
        running_state = jnp.exp(final_state)[:, :, None] * running_state + jnp.einsum('gux,gup->uxp', carried_state, value_block_rows, precision=highest_precision)
        return (running_state, inter_block_output + intra)
    initial = jnp.zeros((heads, width, width), query.dtype)
    _, outputs = lax.scan(jax.checkpoint(block), initial, parts)
    return outputs.reshape(length, heads, width)

def mixer_core(query_raw, forget_raw, value_raw, lower, group_gain, valid):
    length, channels = query_raw.shape
    heads = channels // HEAD
    sigma = jax.nn.sigmoid(forget_raw)
    forget = lower + (1.0 - lower) * sigma
    keep = valid[:, None]
    log_forget = keep * jnp.log(forget)
    key = keep * (1.0 - forget)
    query = jax.nn.silu(query_raw)
    split = (length, heads, HEAD)
    mixed = recurrence(query.reshape(split), log_forget.reshape(split), key.reshape(split), value_raw.reshape(split))
    normed = mixed * lax.rsqrt(lax.optimization_barrier(jnp.mean(mixed * mixed, axis=-1, keepdims=True)) + EPS)
    return normed.reshape(length, channels) * group_gain

def layer(weights, pieces):
    weight_in, weight_out, gate_up, weight_down, vectors = weights
    inputs, valid = pieces
    normed_one = low(rms_norm(inputs, vectors[0]))
    query_raw = low_back(matmul(normed_one, weight_in[0]))
    forget_raw = low_back(matmul(normed_one, weight_in[1]))
    value_raw = low_back(matmul(normed_one, weight_in[2]))
    core = low(mixer_core(query_raw, forget_raw, value_raw, vectors[2], vectors[1], valid))
    mix = low_back(matmul(core, weight_out))
    resid = inputs + mix
    normed_two = low(rms_norm(resid, vectors[3]))
    gate = low_back(matmul(normed_two, gate_up[0]))
    upward = low_back(matmul(normed_two, gate_up[1]))
    hidden = low(jax.nn.silu(gate) * upward)
    ffn = low_back(matmul(hidden, weight_down))
    return (weights, (resid + ffn, mix, ffn))

def moments(first, second, grad):
    first = BETA_ONE * first + (1.0 - BETA_ONE) * grad
    second = BETA_TWO * second + (1.0 - BETA_TWO) * grad * grad
    return (first, second)

def adamw(param, first, second, grad, decay):
    first, second = moments(first, second, grad)
    fix_one = 1.0 - BETA_ONE ** STEP
    fix_two = 1.0 - BETA_TWO ** STEP
    update = first / fix_one / (jnp.sqrt(second / fix_two) + ADAM_EPS) + decay * param
    return (param - LEARN_RATE * update, first, second)

def reference(block_input, cotangent, lengths, vectors, vectors_first, vectors_second, mixer_in, mixer_in_first, mixer_in_second, mixer_out, mixer_out_first, mixer_out_second, ffn_in, ffn_in_first, ffn_in_second, ffn_out, ffn_out_first, ffn_out_second):
    slot_ids = jnp.arange(SLOTS, dtype=jnp.int32)
    valid = (slot_ids[None, :] < lengths.astype(jnp.int32)[:, None]).astype(jnp.float32)
    inputs = block_input.astype(jnp.float32).reshape(SEQS, SLOTS, D)

    def forward(inputs, master_in, master_out, master_gate_up, master_down, vecs):
        weights = (low(master_in), low(master_out), low(master_gate_up), low(master_down), vecs)
        _, outputs = lax.scan(jax.checkpoint(layer), weights, (inputs, valid))
        return outputs
    outputs, pullback = jax.vjp(forward, inputs, mixer_in, mixer_out, ffn_in, ffn_out, vectors)
    total, mix, ffn = outputs
    grad_out = cotangent.astype(jnp.float32).reshape(SEQS, SLOTS, D) * valid[:, :, None]
    grads = pullback((grad_out, jnp.zeros_like(mix), jnp.zeros_like(ffn)))
    grad_x, grad_in, grad_out_w, grad_gate_up, grad_down, grad_vec = grads
    denom = jnp.sum(lengths).astype(jnp.float32) * D
    stats = jnp.stack([jnp.sqrt(jnp.sum(valid[:, :, None] * branch * branch) / denom) for branch in (total, mix, ffn)])
    vec_first, vec_second = moments(vectors_first, vectors_second, grad_vec)
    in_new, in_first, in_second = adamw(mixer_in, mixer_in_first, mixer_in_second, grad_in, DECAY)
    out_new, out_first, out_second = adamw(mixer_out, mixer_out_first, mixer_out_second, grad_out_w, DECAY)
    gu_new, gu_first, gu_second = adamw(ffn_in, ffn_in_first, ffn_in_second, grad_gate_up, DECAY)
    down_new, down_first, down_second = adamw(ffn_out, ffn_out_first, ffn_out_second, grad_down, DECAY)
    return (total.reshape(TOKENS, D).astype(jnp.bfloat16), grad_x.reshape(TOKENS, D), stats, grad_vec, vec_first, vec_second, grad_in, in_new, in_first, in_second, in_new.astype(jnp.bfloat16), grad_out_w, out_new, out_first, out_second, out_new.astype(jnp.bfloat16), grad_gate_up, gu_new, gu_first, gu_second, gu_new.astype(jnp.bfloat16), grad_down, down_new, down_first, down_second, down_new.astype(jnp.bfloat16))
```

```python
import jax
import jax.numpy as jnp
import numpy as np
from jax import lax
from jax.experimental import pallas as pl
from jax.experimental.pallas import tpu as pltpu
from jax.sharding import PartitionSpec as P

HEAD = 128
STEP = 10
CHUNK = 128

EPS = 1e-06
BETA_ONE = 0.9
BETA_TWO = 0.95
DECAY = 0.1
ADAM_EPS = 1e-08
LEARN_RATE = 0.005

NN = ((1,), (0,))
NT = ((1,), (1,))
TN = ((0,), (0,))


def bf16(value):
    return value.astype(jnp.bfloat16)


def f32(value):
    return value.astype(jnp.float32)


def dot(left, right, dims=NN):
    return lax.dot_general(left, right, (dims, ((), ())), preferred_element_type=jnp.float32)


def dot_low(left, right, dims):
    return dot(bf16(left), bf16(right), dims)


def dot_high(left, right, dims):
    left_top, right_top = bf16(left), bf16(right)
    left_rest = bf16(left - f32(left_top))
    right_rest = bf16(right - f32(right_top))
    return (
        dot(left_top, right_top, dims)
        + dot(left_top, right_rest, dims)
        + dot(left_rest, right_top, dims)
    )


def masked_sum(mask, rows, dims):
    top = bf16(rows)
    return dot(mask, top, dims) + dot(mask, bf16(rows - f32(top)), dims)


def gates(forget_raw, lower, keep):
    sigma = jax.nn.sigmoid(forget_raw)
    forget = lower + (1.0 - lower) * sigma
    return sigma, forget, keep * jnp.log(forget), keep * (1.0 - forget)


def causal_mask(rows):
    later = lax.broadcasted_iota(jnp.int32, (rows, rows), 0)
    return later >= lax.broadcasted_iota(jnp.int32, (rows, rows), 1)


def keep_rows(block, rows, length):
    pos = block * rows + lax.broadcasted_iota(jnp.int32, (rows, 1), 0)
    return (pos < length).astype(jnp.float32)


def forward_kernel(length, place, proj, low, gain, core, rec_out, state_out, carry):
    step = pl.program_id(0)
    rows, channels = core.shape

    @pl.when(step == 0)
    def _():
        carry[...] = jnp.zeros_like(carry)

    keep = keep_rows(step, rows, length[0])
    causal = causal_mask(rows)
    ones = causal.astype(jnp.bfloat16)
    for head in range(channels // HEAD):
        cut = pl.ds(head * HEAD, HEAD)
        query_raw = proj[:, cut]
        value = proj[:, pl.ds(2 * channels + head * HEAD, HEAD)]
        lower = low[:, cut]
        forget_raw = proj[:, pl.ds(channels + head * HEAD, HEAD)]
        _, _, logf, key = gates(forget_raw, lower, keep)
        query = query_raw * jax.nn.sigmoid(query_raw)
        run = masked_sum(ones, logf, NN)
        last = run[rows - 1 :, :]
        query_up = query * jnp.exp(run)
        key_down = key * jnp.exp(-run)
        key_tail = key * jnp.exp(last - run)
        state = carry[head]
        state_out[0, head] = state
        scores = jnp.where(causal, dot_low(query_up, key_down, NT), 0.0)
        rec = dot_low(query_up, state, NT) + dot_low(scores, value, NN)
        carry[head] = state * jnp.exp(last) + dot_low(value, key_tail, TN)
        rec_out[:, cut] = rec
        scale = lax.rsqrt(jnp.mean(rec * rec, axis=-1, keepdims=True) + EPS)
        core[:, cut] = bf16(rec * scale * gain[:, cut])


def recurrence_forward(length, place, proj, lower, gain):
    total, wide = proj.shape
    channels = wide // 3
    heads = channels // HEAD
    steps = total // CHUNK
    return pl.pallas_call(
        forward_kernel,
        grid_spec=pltpu.PrefetchScalarGridSpec(
            num_scalar_prefetch=2,
            grid=(steps,),
            in_specs=[
                pl.BlockSpec((CHUNK, wide), lambda i, n, at: (at[i], 0)),
                pl.BlockSpec((1, channels), lambda i, n, at: (0, 0)),
                pl.BlockSpec((1, channels), lambda i, n, at: (0, 0)),
            ],
            out_specs=[
                pl.BlockSpec((CHUNK, channels), lambda i, n, at: (i, 0)),
                pl.BlockSpec((CHUNK, channels), lambda i, n, at: (i, 0)),
                pl.BlockSpec((1, heads, HEAD, HEAD), lambda i, n, at: (i, 0, 0, 0)),
            ],
            scratch_shapes=[pltpu.VMEM((heads, HEAD, HEAD), jnp.float32)],
        ),
        out_shape=[
            jax.ShapeDtypeStruct((total, channels), jnp.bfloat16),
            jax.ShapeDtypeStruct((total, channels), jnp.float32),
            jax.ShapeDtypeStruct((steps, heads, HEAD, HEAD), jnp.float32),
        ],
        compiler_params=pltpu.CompilerParams(vmem_limit_bytes=24 * 1024 * 1024),
        cost_estimate=pl.CostEstimate(
            flops=12 * total * channels * HEAD,
            bytes_accessed=total * channels * 18,
            transcendentals=6 * total * channels,
        ),
        name="recurrence_forward",
    )(length, place, proj, lower, gain)


def backward_kernel(
    length, place, place_core, proj, low, gain, rec_in, state_in, gcore_in, grad, sums, carry, ends
):
    step = pl.program_id(0)
    rows, channels = rec_in.shape

    @pl.when(step == 0)
    def _():
        carry[...] = jnp.zeros_like(carry)
        ends[...] = jnp.zeros_like(ends)
        sums[...] = jnp.zeros_like(sums)

    keep = keep_rows(pl.num_programs(0) - 1 - step, rows, length[0])
    causal = causal_mask(rows)
    ones = causal.astype(jnp.bfloat16)
    for head in range(channels // HEAD):
        cut = pl.ds(head * HEAD, HEAD)
        cut_forget = pl.ds(channels + head * HEAD, HEAD)
        cut_value = pl.ds(2 * channels + head * HEAD, HEAD)
        query_raw = proj[:, cut]
        value = proj[:, cut_value]
        lower = low[:, cut]
        sigma, forget, logf, key = gates(proj[:, cut_forget], lower, keep)
        sig_query = jax.nn.sigmoid(query_raw)
        query = query_raw * sig_query
        run = masked_sum(ones, logf, NN)
        last = run[rows - 1 :, :]
        up = jnp.exp(run)
        down = jnp.exp(-run)
        tail = jnp.exp(last - run)
        query_up = query * up
        key_down = key * down
        key_tail = key * tail
        rec = rec_in[:, cut]
        gcore = f32(gcore_in[:, cut])
        scale = lax.rsqrt(jnp.mean(rec * rec, axis=-1, keepdims=True) + EPS)
        normed = rec * scale
        weighted = gcore * gain[:, cut]
        grec = scale * (weighted - normed * jnp.mean(normed * weighted, axis=-1, keepdims=True))
        state = state_in[0, head]
        after = carry[head]
        scores = jnp.where(causal, dot_low(query_up, key_down, NT), 0.0)
        gscores = jnp.where(causal, dot_high(grec, value, NT), 0.0)
        gquery_up = dot_high(grec, state, NN) + dot_high(gscores, key_down, NN)
        gkey_down = dot_high(gscores, query_up, TN)
        gkey_tail = dot_high(value, after, NN)
        gvalue = dot_low(scores, grec, TN) + dot_low(key_tail, after, NT)
        carry[head] = after * jnp.exp(last) + dot_low(grec, query_up, TN)
        gquery = gquery_up * up
        gkey = gkey_down * down + gkey_tail * tail
        end = jnp.sum(ends[head] * after, axis=0, keepdims=True)
        ends[head] = state
        glogf = masked_sum(ones, query * gquery - key * gkey, TN) + end
        gforget = keep * (glogf / forget - gkey)
        rising = 1.0 - sigma
        grad[:, cut] = bf16(gquery * sig_query * (1.0 + query_raw * (1.0 - sig_query)))
        grad[:, cut_forget] = bf16(gforget * (1.0 - lower) * sigma * rising)
        grad[:, cut_value] = bf16(gvalue)
        sums[0:1, cut] += jnp.sum(gcore * normed, axis=0, keepdims=True)
        sums[1:2, cut] += jnp.sum(gforget * rising, axis=0, keepdims=True)


def recurrence_backward(length, place, place_core, proj, lower, gain, rec, states, gcore):
    total, wide = proj.shape
    channels = wide // 3
    heads = channels // HEAD
    steps = total // CHUNK
    end = steps - 1
    return pl.pallas_call(
        backward_kernel,
        grid_spec=pltpu.PrefetchScalarGridSpec(
            num_scalar_prefetch=3,
            grid=(steps,),
            in_specs=[
                pl.BlockSpec((CHUNK, wide), lambda i, n, at, ac: (at[end - i], 0)),
                pl.BlockSpec((1, channels), lambda i, n, at, ac: (0, 0)),
                pl.BlockSpec((1, channels), lambda i, n, at, ac: (0, 0)),
                pl.BlockSpec((CHUNK, channels), lambda i, n, at, ac: (end - i, 0)),
                pl.BlockSpec((1, heads, HEAD, HEAD), lambda i, n, at, ac: (end - i, 0, 0, 0)),
                pl.BlockSpec((CHUNK, channels), lambda i, n, at, ac: (ac[end - i], 0)),
            ],
            out_specs=[
                pl.BlockSpec((CHUNK, wide), lambda i, n, at, ac: (at[end - i], 0)),
                pl.BlockSpec((8, channels), lambda i, n, at, ac: (0, 0)),
            ],
            scratch_shapes=[
                pltpu.VMEM((heads, HEAD, HEAD), jnp.float32),
                pltpu.VMEM((heads, HEAD, HEAD), jnp.float32),
            ],
        ),
        out_shape=[
            jax.ShapeDtypeStruct((total, wide), jnp.bfloat16),
            jax.ShapeDtypeStruct((8, channels), jnp.float32),
        ],
        compiler_params=pltpu.CompilerParams(vmem_limit_bytes=24 * 1024 * 1024),
        cost_estimate=pl.CostEstimate(
            flops=40 * total * channels * HEAD,
            bytes_accessed=total * channels * 26,
            transcendentals=8 * total * channels,
        ),
        name="recurrence_backward",
    )(length, place, place_core, proj, lower, gain, rec, states, gcore)


class Ring:
    def __init__(self, axis):
        size = lax.axis_size(axis)
        ring = [0, *range(1, size, 2), *range(size - 2, 0, -2)]
        self.axis, self.size = axis, size
        self.ahead = [(ring[i], ring[(i + 1) % size]) for i in range(size)]
        self.back = [(to, start) for start, to in self.ahead]
        rows = np.zeros((size, size), np.int32)
        for at, me in enumerate(ring):
            slots = [me]
            for hop in range(1, size // 2):
                slots += [ring[(at - hop) % size], ring[(at + hop) % size]]
            slots.append(ring[(at + size // 2) % size])
            for slot, owner in enumerate(slots):
                rows[me, owner] = slot
        self.slot_of_owner = rows

    def send(self, value, pairs):
        return lax.ppermute(value, self.axis, pairs)

    def gather(self, own):
        slots, half = [own], own.shape[0] // 2
        one = two = own
        for _ in range(1, self.size // 2):
            one, two = self.send(one, self.ahead), self.send(two, self.back)
            slots += [one, two]
        top, bottom = self.send(one[:half], self.ahead), self.send(two[half:], self.back)
        return [*slots, jnp.concatenate([top, bottom], 0)]

    def scatter(self, parts):
        half = parts[-1].shape[0] // 2
        top = self.send(parts[-1][:half], self.ahead)
        bottom = self.send(parts[-1][half:], self.back)
        one = two = None
        for hop in range(self.size // 2 - 1, 0, -1):
            two, one = (
                parts[2 * hop - 1] if two is None else parts[2 * hop - 1] + two,
                parts[2 * hop] if one is None else parts[2 * hop] + one,
            )
            if top is not None:
                one = jnp.concatenate([one[:half] + top, one[half:]], 0)
                two = jnp.concatenate([two[:half], two[half:] + bottom], 0)
                top = None
            one, two = self.send(one, self.ahead), self.send(two, self.back)
        return f32(parts[0]) + f32(one) + f32(two)


def swap_blocks(axis, blocks):
    size, me = lax.axis_size(axis), lax.axis_index(axis)
    out = [blocks(me)]
    for shift in range(1, size):
        pairs = [(i, (i + shift) % size) for i in range(size)]
        out.append(lax.ppermute(blocks(lax.rem(me + shift, size)), axis, pairs))
    return out


def sum_all(value, axes):
    for axis in axes:
        size, bit = lax.axis_size(axis), 1
        while bit < size:
            value = value + lax.ppermute(value, axis, [(i, i ^ bit) for i in range(size)])
            bit *= 2
    return value


def norm_back(value, scale, gain, grad):
    inner = jnp.mean(value * gain * grad, axis=-1, keepdims=True)
    return scale * gain * grad - value * (scale * scale * scale) * inner


def inverse_rms(value):
    return lax.rsqrt(jnp.mean(value * value, axis=-1, keepdims=True) + EPS)


def moments(first, second, grad):
    first = BETA_ONE * first + (1.0 - BETA_ONE) * grad
    second = BETA_TWO * second + (1.0 - BETA_TWO) * grad * grad
    return (first, second)


def adamw(param, first, second, grad):
    first, second = moments(first, second, grad)
    fix_one = 1.0 - BETA_ONE**STEP
    fix_two = 1.0 - BETA_TWO**STEP
    update = first / fix_one / (jnp.sqrt(second / fix_two) + ADAM_EPS) + DECAY * param
    return (param - LEARN_RATE * update, first, second)


def body(
    block_input,
    cotangent,
    lengths,
    vectors,
    vectors_first,
    vectors_second,
    mixer_in,
    mixer_in_first,
    mixer_in_second,
    mixer_out,
    mixer_out_first,
    mixer_out_second,
    ffn_in,
    ffn_in_first,
    ffn_in_second,
    ffn_out,
    ffn_out_first,
    ffn_out_second,
):
    own_rows, width = block_input.shape
    group = lax.axis_index("dp")
    member = lax.axis_index("mp")
    members = lax.axis_size("mp")
    ring = Ring("mp")
    length = lax.dynamic_index_in_dim(lengths, group, 0, keepdims=True)
    own_pos = member * own_rows + jnp.arange(own_rows, dtype=jnp.int32)
    keep = f32(own_pos < length[0])[:, None]
    channels = mixer_in.shape[2]
    channel_start = member * channels
    group_gain = lax.dynamic_slice_in_dim(vectors[1:2], channel_start, channels, 1)
    lower = lax.dynamic_slice_in_dim(vectors[2:3], channel_start, channels, 1)

    per = own_rows // CHUNK
    blocks = jnp.arange(members * per, dtype=jnp.int32)
    slot = jnp.asarray(ring.slot_of_owner)[member][blocks // per]
    place = slot * per + blocks % per
    place_core = lax.rem(member - blocks // per + members, members) * per + blocks % per

    weight_in = lax.all_gather(bf16(mixer_in), "dp", axis=1, tiled=True)
    weight_out = lax.all_gather(bf16(mixer_out), "mp", axis=0, tiled=True)
    weight_out = lax.all_gather(weight_out, "dp", axis=1, tiled=True)
    weight_gate_up = lax.all_gather(bf16(ffn_in), "dp", axis=1, tiled=True)
    weight_down = lax.all_gather(bf16(ffn_out), "dp", axis=1, tiled=True)

    inputs = f32(block_input)
    scale_one = inverse_rms(inputs)
    normed_one = ring.gather(bf16(inputs * scale_one * vectors[0]))
    proj = jnp.concatenate(
        [jnp.concatenate([dot(rows, weight_in[j]) for j in range(3)], 1) for rows in normed_one], 0
    )
    core, rec, states = recurrence_forward(length, place, proj, lower, group_gain)
    core_own = swap_blocks(
        "mp", lambda owner: lax.dynamic_slice_in_dim(core, owner * own_rows, own_rows, 0)
    )

    def out_rows(shift):
        start = lax.rem(member - shift + members, members) * channels
        return lax.dynamic_slice_in_dim(weight_out, start, channels, 0)

    mix = sum(dot(part, out_rows(shift)) for shift, part in enumerate(core_own))
    resid = inputs + mix
    scale_two = inverse_rms(resid)

    grad_total = f32(cotangent) * keep
    grad_rows = ring.gather(bf16(grad_total))
    normed_two = ring.gather(bf16(resid * scale_two * vectors[3]))
    hidden, grad_gate, grad_up, ffn_parts, two_parts = [], [], [], [], []
    for rows, grows in zip(normed_two, grad_rows):
        gate, up = dot(rows, weight_gate_up[0]), dot(rows, weight_gate_up[1])
        sigma = jax.nn.sigmoid(gate)
        act = gate * sigma
        hidden.append(bf16(act * up))
        ghid = dot(grows, weight_down, NT)
        grad_gate.append(bf16(ghid * up * sigma * (1.0 + gate * (1.0 - sigma))))
        grad_up.append(bf16(ghid * act))
        two_parts.append(
            bf16(
                dot(grad_gate[-1], weight_gate_up[0], NT) + dot(grad_up[-1], weight_gate_up[1], NT)
            )
        )
        ffn_parts.append(bf16(dot(hidden[-1], weight_down)))
    grad_two = ring.scatter(two_parts)
    ffn = ring.scatter(ffn_parts)
    total = resid + ffn
    grad_resid = grad_total + norm_back(resid, scale_two, vectors[3], grad_two)
    gain_two = jnp.sum(grad_two * resid * scale_two, axis=0)

    grad_mix = bf16(grad_resid)
    grad_core = bf16(dot(grad_mix, weight_out, NT))
    grad_core = jnp.concatenate(
        swap_blocks(
            "mp", lambda owner: lax.dynamic_slice_in_dim(grad_core, owner * channels, channels, 1)
        ),
        0,
    )
    grad_proj, sums = recurrence_backward(
        length, place, place_core, proj, lower, group_gain, rec, states, grad_core
    )
    grad_proj_slots = [
        grad_proj[i * own_rows : (i + 1) * own_rows] for i in range(members)
    ]
    one_parts = [
        bf16(
            sum(
                dot(rows[:, j * channels : (j + 1) * channels], weight_in[j], NT) for j in range(3)
            )
        )
        for rows in grad_proj_slots
    ]
    normed_one_all = jnp.concatenate(normed_one, 0)
    sum_in = jnp.stack(
        [
            bf16(dot(normed_one_all, grad_proj[:, j * channels : (j + 1) * channels], TN))
            for j in range(3)
        ]
    )
    grad_one = ring.scatter(one_parts)
    input_grad = grad_resid + norm_back(inputs, scale_one, vectors[0], grad_one)
    gain_one = jnp.sum(grad_one * inputs * scale_one, axis=0)

    grad_all = jnp.concatenate(grad_rows, 0)
    normed_two_all = jnp.concatenate(normed_two, 0)
    sum_down = bf16(dot(jnp.concatenate(hidden, 0), grad_all, TN))
    sum_gate = bf16(dot(normed_two_all, jnp.concatenate(grad_gate, 0), TN))
    sum_up = bf16(dot(normed_two_all, jnp.concatenate(grad_up, 0), TN))
    core_rows = jnp.concatenate(core_own, 1)
    sum_out = bf16(dot(core_rows, grad_mix, TN))
    order = [lax.rem(member - q + members, members) * channels for q in range(members)]
    sum_out = jnp.concatenate(
        [lax.dynamic_slice_in_dim(sum_out, at, channels, 0) for at in order], 0
    )

    def owned(value, axis, name="dp"):
        return lax.psum_scatter(value, name, scatter_dimension=axis, tiled=True)

    shard_down = f32(owned(sum_down, 1))
    shard_gate_up = jnp.stack([f32(owned(sum_gate, 0)), f32(owned(sum_up, 0))])
    shard_out = f32(owned(owned(sum_out, 1), 0, "mp"))
    shard_in = f32(owned(sum_in, 1))

    blank = jnp.zeros((width,), jnp.float32)
    squares = jnp.stack([jnp.sum(keep * part * part) for part in (total, mix, ffn)])
    vector_part = jnp.stack(
        [
            gain_one,
            lax.dynamic_update_slice_in_dim(blank, sums[0], channel_start, 0),
            lax.dynamic_update_slice_in_dim(blank, sums[1], channel_start, 0),
            gain_two,
            lax.dynamic_update_slice_in_dim(blank, squares, 0, 0),
        ]
    )
    vector_sums = sum_all(vector_part, ("dp", "mp"))
    vectors_grad = vector_sums[:4]
    denom = f32(jnp.sum(lengths)) * width
    stats = jnp.sqrt(vector_sums[4, :3] / denom)
    vec_first, vec_second = moments(vectors_first, vectors_second, vectors_grad)

    in_new, in_first, in_second = adamw(mixer_in, mixer_in_first, mixer_in_second, shard_in)
    out_new, out_first, out_second = adamw(mixer_out, mixer_out_first, mixer_out_second, shard_out)
    gu_new, gu_first, gu_second = adamw(ffn_in, ffn_in_first, ffn_in_second, shard_gate_up)
    down_new, down_first, down_second = adamw(ffn_out, ffn_out_first, ffn_out_second, shard_down)
    in_low, out_low, gu_low, down_low = (
        lax.all_gather(bf16(new), "dp", axis=1, tiled=True)
        for new in (in_new, out_new, gu_new, down_new)
    )
    return (
        bf16(total),
        input_grad,
        stats,
        vectors_grad,
        vec_first,
        vec_second,
        shard_in,
        in_new,
        in_first,
        in_second,
        in_low,
        shard_out,
        out_new,
        out_first,
        out_second,
        out_low,
        shard_gate_up,
        gu_new,
        gu_first,
        gu_second,
        gu_low,
        shard_down,
        down_new,
        down_first,
        down_second,
        down_low,
    )


def solution(mesh):
    rows = P(("dp", "mp"), None)
    deep = P(None, "dp", "mp")
    flat = P("mp", "dp")
    in_specs = (
        (rows, rows, P(), P(), P(), P()) + (deep,) * 3 + (flat,) * 3 + (deep,) * 3 + (flat,) * 3
    )
    wide = (deep,) * 4 + (P(None, None, "mp"),)
    tall = (flat,) * 4 + (P("mp", None),)
    out_specs = (rows, rows, P(), P(), P(), P()) + wide + tall + wide + tall
    return jax.shard_map(body, mesh=mesh, in_specs=in_specs, out_specs=out_specs, check_vma=False)
```

```python
import functools

import jax
import jax.numpy as jnp
import numpy as np
from jax import lax
from jax.experimental import pallas as pl
from jax.experimental.pallas import tpu as pltpu
from jax.sharding import PartitionSpec as P

HEAD = 128
STEP = 10
CHUNK = 128

EPS = 1e-06
BETA_ONE = 0.9
BETA_TWO = 0.95
DECAY = 0.1
ADAM_EPS = 1e-08
LEARN_RATE = 0.005

NN = ((1,), (0,))
NT = ((1,), (1,))
TN = ((0,), (0,))


def bf16(value):
    return value.astype(jnp.bfloat16)


def f32(value):
    return value.astype(jnp.float32)


def dot(left, right, dims=NN):
    return lax.dot_general(left, right, (dims, ((), ())), preferred_element_type=jnp.float32)


def dot_low(left, right, dims):
    return dot(bf16(left), bf16(right), dims)


def dot_high(left, right, dims):
    left_top, right_top = bf16(left), bf16(right)
    left_rest = bf16(left - f32(left_top))
    right_rest = bf16(right - f32(right_top))
    return (
        dot(left_top, right_top, dims)
        + dot(left_top, right_rest, dims)
        + dot(left_rest, right_top, dims)
    )


def masked_sum(mask, rows, dims):
    top = bf16(rows)
    return dot(mask, top, dims) + dot(mask, bf16(rows - f32(top)), dims)


def gates(forget_raw, lower, keep):
    sigma = jax.nn.sigmoid(forget_raw)
    forget = lower + (1.0 - lower) * sigma
    return sigma, forget, keep * jnp.log(forget), keep * (1.0 - forget)


def causal_mask(rows):
    later = lax.broadcasted_iota(jnp.int32, (rows, rows), 0)
    return later >= lax.broadcasted_iota(jnp.int32, (rows, rows), 1)


def keep_rows(block, rows, length):
    pos = block * rows + lax.broadcasted_iota(jnp.int32, (rows, 1), 0)
    return (pos < length).astype(jnp.float32)


def forward_kernel(count, length, slot, part, core_at, *refs):
    parts, refs = refs[:count], refs[-7:]
    low, gain, core, rec_out, state_out, proj, carry = refs
    step = pl.program_id(0)
    rows, channels = core.shape

    @pl.when(step == 0)
    def _():
        carry[...] = jnp.zeros_like(carry)

    for index in range(count):

        @pl.when(slot[step] == index)
        def _(index=index):
            proj[...] = parts[index][...]

    keep = keep_rows(step, rows, length[0])
    causal = causal_mask(rows)
    ones = causal.astype(jnp.bfloat16)
    for head in range(channels // HEAD):
        cut = pl.ds(head * HEAD, HEAD)
        query_raw = proj[:, cut]
        value = proj[:, pl.ds(2 * channels + head * HEAD, HEAD)]
        lower = low[:, cut]
        forget_raw = proj[:, pl.ds(channels + head * HEAD, HEAD)]
        _, _, logf, key = gates(forget_raw, lower, keep)
        query = query_raw * jax.nn.sigmoid(query_raw)
        run = masked_sum(ones, logf, NN)
        last = run[rows - 1 :, :]
        query_up = query * jnp.exp(run)
        key_down = key * jnp.exp(-run)
        key_tail = key * jnp.exp(last - run)
        state = carry[head]
        state_out[0, head] = state
        scores = jnp.where(causal, dot_low(query_up, key_down, NT), 0.0)
        rec = dot_low(query_up, state, NT) + dot_low(scores, value, NN)
        carry[head] = state * jnp.exp(last) + dot_low(value, key_tail, TN)
        rec_out[:, cut] = rec
        scale = lax.rsqrt(jnp.mean(rec * rec, axis=-1, keepdims=True) + EPS)
        core[:, cut] = bf16(rec * scale * gain[:, cut])


def part_spec(index, wide, last):
    return pl.BlockSpec((CHUNK, wide), lambda i, n, slot, part, *_: (part[index * (last + 1) + i], 0))


def recurrence_forward(length, slot, part, core_at, parts, lower, gain, needed):
    wide = parts[0].shape[1]
    total = len(parts) * parts[0].shape[0]
    channels = wide // 3
    heads = channels // HEAD
    steps = total // CHUNK
    return pl.pallas_call(
        functools.partial(forward_kernel, len(parts)),
        grid_spec=pltpu.PrefetchScalarGridSpec(
            num_scalar_prefetch=4,
            grid=(steps,),
            in_specs=[
                *(part_spec(index, wide, steps - 1) for index in range(len(parts))),
                *(pl.BlockSpec(memory_space=pl.ANY) for _ in needed),
                pl.BlockSpec((1, channels), lambda i, *_: (0, 0)),
                pl.BlockSpec((1, channels), lambda i, *_: (0, 0)),
            ],
            out_specs=[
                pl.BlockSpec((CHUNK, channels), lambda i, n, slot, part, at: (at[i], 0)),
                pl.BlockSpec((CHUNK, channels), lambda i, *_: (i, 0)),
                pl.BlockSpec((1, heads, HEAD, HEAD), lambda i, *_: (i, 0, 0, 0)),
            ],
            scratch_shapes=[
                pltpu.VMEM((CHUNK, wide), jnp.float32),
                pltpu.VMEM((heads, HEAD, HEAD), jnp.float32),
            ],
        ),
        out_shape=[
            jax.ShapeDtypeStruct((total, channels), jnp.bfloat16),
            jax.ShapeDtypeStruct((total, channels), jnp.float32),
            jax.ShapeDtypeStruct((steps, heads, HEAD, HEAD), jnp.float32),
        ],
        compiler_params=pltpu.CompilerParams(vmem_limit_bytes=32 * 1024 * 1024),
        cost_estimate=pl.CostEstimate(
            flops=12 * total * channels * HEAD,
            bytes_accessed=total * channels * 18,
            transcendentals=6 * total * channels,
        ),
        name="recurrence_forward",
    )(length, slot, part, core_at, *parts, *needed, lower, gain)


def backward_kernel(count, length, slot, part, place, slot_core, part_core, *refs):
    parts, gcores, refs = refs[:count], refs[count : 2 * count], refs[-10:]
    low, gain, rec_in, state_in, grad, sums, proj, gcore_in, carry, ends = refs
    step = pl.program_id(0)
    rows, channels = rec_in.shape

    for index in range(count):

        @pl.when(slot[pl.num_programs(0) - 1 - step] == index)
        def _(index=index):
            proj[...] = parts[index][...]

        @pl.when(slot_core[pl.num_programs(0) - 1 - step] == index)
        def _(index=index):
            gcore_in[...] = f32(gcores[index][...])

    @pl.when(step == 0)
    def _():
        carry[...] = jnp.zeros_like(carry)
        ends[...] = jnp.zeros_like(ends)
        sums[...] = jnp.zeros_like(sums)

    keep = keep_rows(pl.num_programs(0) - 1 - step, rows, length[0])
    causal = causal_mask(rows)
    ones = causal.astype(jnp.bfloat16)
    for head in range(channels // HEAD):
        cut = pl.ds(head * HEAD, HEAD)
        cut_forget = pl.ds(channels + head * HEAD, HEAD)
        cut_value = pl.ds(2 * channels + head * HEAD, HEAD)
        query_raw = proj[:, cut]
        value = proj[:, cut_value]
        lower = low[:, cut]
        sigma, forget, logf, key = gates(proj[:, cut_forget], lower, keep)
        sig_query = jax.nn.sigmoid(query_raw)
        query = query_raw * sig_query
        run = masked_sum(ones, logf, NN)
        last = run[rows - 1 :, :]
        up = jnp.exp(run)
        down = jnp.exp(-run)
        tail = jnp.exp(last - run)
        query_up = query * up
        key_down = key * down
        key_tail = key * tail
        rec = rec_in[:, cut]
        gcore = gcore_in[:, cut]
        scale = lax.rsqrt(jnp.mean(rec * rec, axis=-1, keepdims=True) + EPS)
        normed = rec * scale
        weighted = gcore * gain[:, cut]
        grec = scale * (weighted - normed * jnp.mean(normed * weighted, axis=-1, keepdims=True))
        state = state_in[0, head]
        after = carry[head]
        scores = jnp.where(causal, dot_low(query_up, key_down, NT), 0.0)
        gscores = jnp.where(causal, dot_high(grec, value, NT), 0.0)
        gquery_up = dot_high(grec, state, NN) + dot_high(gscores, key_down, NN)
        gkey_down = dot_high(gscores, query_up, TN)
        gkey_tail = dot_high(value, after, NN)
        gvalue = dot_low(scores, grec, TN) + dot_low(key_tail, after, NT)
        carry[head] = after * jnp.exp(last) + dot_low(grec, query_up, TN)
        gquery = gquery_up * up
        gkey = gkey_down * down + gkey_tail * tail
        end = jnp.sum(ends[head] * after, axis=0, keepdims=True)
        ends[head] = state
        glogf = masked_sum(ones, query * gquery - key * gkey, TN) + end
        gforget = keep * (glogf / forget - gkey)
        rising = 1.0 - sigma
        grad[:, cut] = bf16(gquery * sig_query * (1.0 + query_raw * (1.0 - sig_query)))
        grad[:, cut_forget] = bf16(gforget * (1.0 - lower) * sigma * rising)
        grad[:, cut_value] = bf16(gvalue)
        sums[0:1, cut] += jnp.sum(gcore * normed, axis=0, keepdims=True)
        sums[1:2, cut] += jnp.sum(gforget * rising, axis=0, keepdims=True)


def recurrence_backward(length, tables, parts, gcores, lower, gain, rec, states, needed):
    wide = parts[0].shape[1]
    total = len(parts) * parts[0].shape[0]
    channels = wide // 3
    heads = channels // HEAD
    steps = total // CHUNK
    end = steps - 1

    def proj_spec(index):
        return pl.BlockSpec(
            (CHUNK, wide), lambda i, n, slot, part, *_: (part[index * steps + end - i], 0)
        )

    def core_spec(index):
        return pl.BlockSpec(
            (CHUNK, channels),
            lambda i, n, slot, part, place, sc, pc: (pc[index * steps + end - i], 0),
        )

    return pl.pallas_call(
        functools.partial(backward_kernel, len(parts)),
        grid_spec=pltpu.PrefetchScalarGridSpec(
            num_scalar_prefetch=6,
            grid=(steps,),
            in_specs=[
                *(proj_spec(index) for index in range(len(parts))),
                *(core_spec(index) for index in range(len(parts))),
                *(pl.BlockSpec(memory_space=pl.ANY) for _ in needed),
                pl.BlockSpec((1, channels), lambda i, *_: (0, 0)),
                pl.BlockSpec((1, channels), lambda i, *_: (0, 0)),
                pl.BlockSpec((CHUNK, channels), lambda i, *_: (end - i, 0)),
                pl.BlockSpec((1, heads, HEAD, HEAD), lambda i, *_: (end - i, 0, 0, 0)),
            ],
            out_specs=[
                pl.BlockSpec((CHUNK, wide), lambda i, n, slot, part, place, *_: (place[end - i], 0)),
                pl.BlockSpec((8, channels), lambda i, *_: (0, 0)),
            ],
            scratch_shapes=[
                pltpu.VMEM((CHUNK, wide), jnp.float32),
                pltpu.VMEM((CHUNK, channels), jnp.float32),
                pltpu.VMEM((heads, HEAD, HEAD), jnp.float32),
                pltpu.VMEM((heads, HEAD, HEAD), jnp.float32),
            ],
        ),
        out_shape=[
            jax.ShapeDtypeStruct((total, wide), jnp.bfloat16),
            jax.ShapeDtypeStruct((8, channels), jnp.float32),
        ],
        compiler_params=pltpu.CompilerParams(vmem_limit_bytes=32 * 1024 * 1024),
        cost_estimate=pl.CostEstimate(
            flops=40 * total * channels * HEAD,
            bytes_accessed=total * channels * 26,
            transcendentals=8 * total * channels,
        ),
        name="recurrence_backward",
    )(length, *tables, *parts, *gcores, *needed, lower, gain, rec, states)


class Ring:
    def __init__(self, axis):
        size = lax.axis_size(axis)
        ring = [0, *range(1, size, 2), *range(size - 2, 0, -2)]
        self.axis, self.size = axis, size
        self.ahead = [(ring[i], ring[(i + 1) % size]) for i in range(size)]
        self.owner_of_slot = np.zeros((size, size), np.int32)
        for at, me in enumerate(ring):
            self.owner_of_slot[me] = [ring[at - slot] for slot in range(size)]

    def send(self, value):
        return lax.ppermute(value, self.axis, self.ahead)

    def gather(self, own, held=lambda slots: ()):
        slots = [own]
        for _ in range(1, self.size):
            got = self.send(slots[-1])
            slots.append(after(got, *held(slots)))
        return slots

    def scatter(self, parts):
        total = self.send(parts[1])
        for step in range(2, self.size):
            needed = (yield total) or ()
            total = self.send(bf16(f32(after(parts[step], *needed)) + f32(total)))
        needed = (yield total) or ()
        yield f32(after(parts[0], *needed)) + f32(total)


def flip(value, axis, bit):
    return lax.ppermute(value, axis, [(i, i ^ (1 << bit)) for i in range(lax.axis_size(axis))])


class Halving:
    def __init__(self, value, axis, order):
        size = lax.axis_size(axis)
        bits = size.bit_length() - 1
        self.axis, self.order, self.left = axis, list(order), list(range(bits - 1, -1, -1))
        self.value = value.reshape((2,) * bits + (value.shape[0] // size, value.shape[1]))

    def step(self, *needed):
        bit = self.order.pop(0)
        at, mine = self.left.index(bit), (lax.axis_index(self.axis) >> bit) & 1
        sent = lax.dynamic_index_in_dim(self.value, 1 - mine, at, keepdims=False)
        kept = lax.dynamic_index_in_dim(self.value, mine, at, keepdims=False)
        got = flip(after(sent, *needed), self.axis, bit)
        self.left.pop(at)
        total = f32(kept) + f32(got)
        self.value = bf16(total) if self.order else total
        return got


class HalvingColumns:
    def __init__(self, value, axis, order):
        self.axis, self.order, self.value = axis, list(order), value

    def step(self, *needed):
        bit, half = self.order.pop(0), self.value.shape[1] // 2
        got = flip(after(self.value[:, half:], *needed), self.axis, bit)
        total = f32(self.value[:, :half]) + f32(got)
        self.value = bf16(total) if self.order else total
        return got


def after(value, *needed):
    return lax.optimization_barrier((value, needed))[0] if needed else value


def behind(value, mark):
    return jnp.where(mark > 3.0e38, mark, value)


def permute_kernel(blocks, order, value, out):
    block = value.shape[1] // blocks
    for i in range(blocks):
        cut = pl.ds(pl.multiple_of(order[i] * block, block), block)
        out[:, pl.ds(i * block, block)] = value[:, cut]


def permute_columns(value, order):
    blocks = order.shape[0]
    whole = pl.BlockSpec(value.shape, lambda i, *_: (0, 0))
    return pl.pallas_call(
        functools.partial(permute_kernel, blocks),
        grid_spec=pltpu.PrefetchScalarGridSpec(
            num_scalar_prefetch=1, grid=(1,), in_specs=[whole], out_specs=whole
        ),
        out_shape=jax.ShapeDtypeStruct(value.shape, value.dtype),
        name="permute_columns",
    )(order, value)


def column_order(axis, order):
    size, me = lax.axis_size(axis), lax.axis_index(axis)
    bits = size.bit_length() - 1
    offsets = [
        sum(((at >> (bits - 1 - i)) & 1) << bit for i, bit in enumerate(order)) for at in range(size)
    ]
    return jnp.asarray(np.array(offsets, np.int32)) ^ me.astype(jnp.int32)


def bit_orders(axis):
    upper = list(range(1, lax.axis_size(axis).bit_length() - 1))
    return [0, *upper], [0, *upper[::-1]]


def sum_all(value, axes):
    for axis in axes:
        for bit in range(lax.axis_size(axis).bit_length() - 1):
            value = value + flip(value, axis, bit)
    return value


def copy_kernel(value, out):
    out[...] = value[...]


def copied(value):
    outer, rows, width = value.shape
    spec = pl.BlockSpec((1, rows // 4, width), lambda i, j: (i, j, 0))
    return pl.pallas_call(
        copy_kernel,
        grid=(outer, 4),
        in_specs=[spec],
        out_specs=spec,
        out_shape=jax.ShapeDtypeStruct(value.shape, value.dtype),
        name="copied",
    )(value)


def by_slot(value, size):
    rows = value.shape[0] // size
    return [value[slot * rows : (slot + 1) * rows] for slot in range(size)]


def norm_back(value, scale, gain, grad):
    inner = jnp.mean(value * gain * grad, axis=-1, keepdims=True)
    return scale * gain * grad - value * (scale * scale * scale) * inner


def inverse_rms(value):
    return lax.rsqrt(jnp.mean(value * value, axis=-1, keepdims=True) + EPS)


def moments(first, second, grad):
    first = BETA_ONE * first + (1.0 - BETA_ONE) * grad
    second = BETA_TWO * second + (1.0 - BETA_TWO) * grad * grad
    return (first, second)


def adamw(param, first, second, grad):
    first, second = moments(first, second, grad)
    fix_one = 1.0 - BETA_ONE**STEP
    fix_two = 1.0 - BETA_TWO**STEP
    update = first / fix_one / (jnp.sqrt(second / fix_two) + ADAM_EPS) + DECAY * param
    return (param - LEARN_RATE * update, first, second)


def body(
    block_input,
    cotangent,
    lengths,
    vectors,
    vectors_first,
    vectors_second,
    mixer_in,
    mixer_in_first,
    mixer_in_second,
    mixer_out,
    mixer_out_first,
    mixer_out_second,
    ffn_in,
    ffn_in_first,
    ffn_in_second,
    ffn_out,
    ffn_out_first,
    ffn_out_second,
):
    own_rows, width = block_input.shape
    group = lax.axis_index("dp")
    member = lax.axis_index("mp")
    members = lax.axis_size("mp")
    ring = Ring("mp")
    length = lax.dynamic_index_in_dim(lengths, group, 0, keepdims=True)
    own_pos = member * own_rows + jnp.arange(own_rows, dtype=jnp.int32)
    keep = f32(own_pos < length[0])[:, None]
    channels = mixer_in.shape[2]
    channel_start = member * channels
    group_gain = lax.dynamic_slice_in_dim(vectors[1:2], channel_start, channels, 1)
    lower = lax.dynamic_slice_in_dim(vectors[2:3], channel_start, channels, 1)

    per = own_rows // CHUNK
    blocks = jnp.arange(members * per, dtype=jnp.int32)
    owner_of_slot = jnp.asarray(ring.owner_of_slot)[member]
    slot = jnp.asarray(np.argsort(ring.owner_of_slot, 1).astype(np.int32))[member][blocks // per]
    part = jnp.clip(blocks[None, :] - owner_of_slot[:, None] * per, 0, per - 1).reshape(-1)
    place = slot * per + blocks % per

    in_shard = jnp.concatenate([bf16(mixer_in[j]) for j in range(3)], 1)
    half_in = 3 * channels // 2
    halves_in = (slice(0, half_in), slice(half_in, None))
    order_one, order_two = bit_orders("dp")
    inputs = f32(block_input)
    scale_one = inverse_rms(inputs)
    own_one = bf16(inputs * scale_one * vectors[0])
    weight_in = lax.all_gather(in_shard, "dp", axis=0, tiled=True)
    order_out = column_order("dp", order_one)
    weight_out = lax.all_gather(bf16(mixer_out), "dp", axis=1, tiled=True)
    weight_gate_up = lax.all_gather(bf16(ffn_in), "dp", axis=1, tiled=True)
    weight_down = lax.all_gather(bf16(ffn_out), "dp", axis=1, tiled=True)
    proj = []

    def project(slots):
        if len(slots) > 2:
            proj.append(dot(slots[len(proj)], weight_in))
        return proj[-1:]

    normed_one = ring.gather(own_one, project)
    while len(proj) < members:
        project(normed_one)

    grad_total = f32(cotangent) * keep
    grad_rows = ring.gather(after(bf16(grad_total), normed_one[-1]))
    core, rec, states = recurrence_forward(length, slot, part, place, proj, lower, group_gain, ())
    mix_parts = by_slot(bf16(dot(core, weight_out)), members)
    mix_parts[1] = after(mix_parts[1], grad_rows[1])
    steps = ring.scatter(mix_parts)
    for _ in range(members - 1):
        next(steps)
    mix = next(steps)
    resid = inputs + mix
    scale_two = inverse_rms(resid)

    hidden, grad_gate, grad_up, two_parts = [], [], [], []

    def feed(slots):
        rows, grows = slots[-1], grad_rows[len(slots) - 1]
        gate, up = dot(rows, weight_gate_up[0]), dot(rows, weight_gate_up[1])
        sigma = jax.nn.sigmoid(gate)
        act = gate * sigma
        hidden.append(bf16(act * up))
        ghid = dot(grows, weight_down, NT)
        grad_gate.append(bf16(ghid * up * sigma * (1.0 + gate * (1.0 - sigma))))
        grad_up.append(bf16(ghid * act))
        two_parts.append(
            bf16(
                dot(grad_gate[-1], weight_gate_up[0], NT) + dot(grad_up[-1], weight_gate_up[1], NT)
            )
        )
        return two_parts[-1:]

    normed_two = ring.gather(bf16(resid * scale_two * vectors[3]), feed)
    steps = ring.scatter(two_parts)
    normed_two[-1] = after(normed_two[-1], next(steps))
    feed(normed_two)
    for _ in range(members - 4):
        steps.send(())
    came = steps.send(())
    normed_two_all = jnp.concatenate(normed_two, 0)
    sum_gate_up = jnp.stack(
        [
            bf16(dot(normed_two_all, after(jnp.concatenate(part, 0), *two_parts), TN))
            for part in (grad_gate, grad_up)
        ]
    )
    shard_gate_up = lax.psum_scatter(sum_gate_up, "dp", scatter_dimension=1, tiled=True)
    hidden_all = after(jnp.concatenate(hidden, 0), came)
    sum_down = bf16(dot(hidden_all, jnp.concatenate(grad_rows, 0), TN))
    shard_down = lax.psum_scatter(sum_down, "dp", scatter_dimension=1, tiled=True)
    ffn_parts = by_slot(bf16(dot(hidden_all, weight_down)), members)
    steps.send(())
    grad_two = steps.send((sum_gate_up,))

    grad_resid = grad_total + norm_back(resid, scale_two, vectors[3], grad_two)
    gain_two = jnp.sum(grad_two * resid * scale_two, axis=0)

    weight_out = permute_columns(weight_out, order_out)
    grad_core = []

    def pull(slots):
        grad_core.append(bf16(dot(slots[-1], weight_out, NT)))
        return [*grad_core[-1:], *ffn_parts[: len(slots) // 2]]

    grad_mix = ring.gather(permute_columns(bf16(grad_resid), order_out), pull)
    grad_core.append(bf16(dot(grad_mix[-1], weight_out, NT)))
    grad_proj, sums = recurrence_backward(
        length,
        (slot, part, place, slot, part),
        proj,
        grad_core,
        lower,
        group_gain,
        rec,
        states,
        (),
    )
    sum_out = bf16(dot(core, jnp.concatenate(grad_mix, 0), TN))
    out_sum = HalvingColumns(sum_out, "dp", order_one)
    shard_gate_up = behind(f32(shard_gate_up), sums[0, 0])
    gu_new, gu_first, gu_second = adamw(ffn_in, ffn_in_first, ffn_in_second, shard_gate_up)
    gu_sent = bf16(gu_new)

    ffn_parts[1] = after(ffn_parts[1], grad_mix[-1])
    steps = ring.scatter(ffn_parts)
    one = next(steps)
    done = [out_sum.step(grad_mix[-1])]

    two = steps.send((grad_proj, *done))
    grad_proj = after(grad_proj, one)
    normed_one_all = jnp.concatenate(normed_one, 0)
    sum_in = [bf16(dot(normed_one_all, grad_proj[:, cut], TN)) for cut in halves_in]
    in_sums = [Halving(piece, "dp", order) for piece, order in zip(sum_in, (order_one, order_two))]
    done = [out_sum.step(one), *(item.step() for item in in_sums)]

    shard_down = behind(f32(shard_down), sums[0, 0])
    down_new, down_first, down_second = adamw(ffn_out, ffn_out_first, ffn_out_second, shard_down)
    down_sent = bf16(down_new)

    three = steps.send((*sum_in, gu_sent))
    grad_proj = after(grad_proj, two)
    one_parts = by_slot(bf16(dot(grad_proj, weight_in, NT)), members)
    done += [item.step(two) for item in in_sums]
    while out_sum.order:
        done.append(out_sum.step(two))
    for _ in range(members - 4):
        three = steps.send(())
    ffn = steps.send((*one_parts, *done, down_sent))
    total = resid + ffn
    one_parts[1] = after(one_parts[1], ffn)

    steps = ring.scatter(one_parts)
    one = next(steps)
    while in_sums[0].order:
        done = [item.step(three) for item in in_sums]
    shard_out = after(out_sum.value, three)
    out_new, out_first, out_second = adamw(mixer_out, mixer_out_first, mixer_out_second, shard_out)
    out_sent = bf16(out_new)
    gain_one = sum(
        jnp.sum(f32(weight_in[:, cut]) * f32(piece), axis=1)
        for cut, piece in zip(halves_in, after(sum_in, three))
    )
    blank = jnp.zeros((width,), jnp.float32)
    squares = jnp.stack([jnp.sum(keep * piece * piece) for piece in (total, mix, ffn)])
    vector_part = jnp.stack(
        [
            gain_one / vectors[0],
            lax.dynamic_update_slice_in_dim(blank, sums[0], channel_start, 0),
            lax.dynamic_update_slice_in_dim(blank, sums[1], channel_start, 0),
            gain_two,
            lax.dynamic_update_slice_in_dim(blank, squares, 0, 0),
        ]
    )


    two = steps.send((vector_part, out_sent, *done))
    shard_in = jnp.concatenate([after(item.value, one) for item in in_sums], 1)
    shard_in = jnp.stack([shard_in[:, j * channels : (j + 1) * channels] for j in range(3)])
    in_new, in_first, in_second = adamw(mixer_in, mixer_in_first, mixer_in_second, shard_in)
    in_sent = bf16(in_new)
    vector_sums = sum_all(after(vector_part, one), ("dp",))

    gu_low = copied(lax.all_gather(gu_sent, "dp", axis=1, tiled=True))
    one_parts[-1] = behind(one_parts[-1], gu_low[0, 0, 0])
    three = steps.send((in_sent, vector_sums))
    for _ in range(members - 4):
        three = steps.send(())
    grad_one = steps.send(())
    vector_sums = sum_all(after(vector_sums, three), ("mp",))
    input_grad = grad_resid + norm_back(inputs, scale_one, vectors[0], grad_one)
    vectors_grad = vector_sums[:4]
    denom = f32(jnp.sum(lengths)) * width
    stats = jnp.sqrt(vector_sums[4, :3] / denom)
    vec_first, vec_second = moments(vectors_first, vectors_second, vectors_grad)

    down_low, out_low, in_low = (
        lax.all_gather(new, "dp", axis=1, tiled=True) for new in (down_sent, out_sent, in_sent)
    )
    return (
        bf16(total),
        input_grad,
        stats,
        vectors_grad,
        vec_first,
        vec_second,
        shard_in,
        in_new,
        in_first,
        in_second,
        in_low,
        shard_out,
        out_new,
        out_first,
        out_second,
        out_low,
        shard_gate_up,
        gu_new,
        gu_first,
        gu_second,
        gu_low,
        shard_down,
        down_new,
        down_first,
        down_second,
        down_low,
    )


def solution(mesh):
    rows = P(("dp", "mp"), None)
    deep = P(None, "dp", "mp")
    flat = P("mp", "dp")
    in_specs = (
        (rows, rows, P(), P(), P(), P()) + (deep,) * 3 + (flat,) * 3 + (deep,) * 3 + (flat,) * 3
    )
    wide = (deep,) * 4 + (P(None, None, "mp"),)
    tall = (flat,) * 4 + (P("mp", None),)
    out_specs = (rows, rows, P(), P(), P(), P()) + wide + tall + wide + tall
    return jax.shard_map(body, mesh=mesh, in_specs=in_specs, out_specs=out_specs, check_vma=False)
```

```python
import functools

import jax
import jax.numpy as jnp
import numpy as np
from jax import lax
from jax.experimental import pallas as pl
from jax.experimental.pallas import tpu as pltpu
from jax.sharding import PartitionSpec as P

HEAD = 128
STEP = 10
CHUNK = 128

EPS = 1e-06
BETA_ONE = 0.9
BETA_TWO = 0.95
DECAY = 0.1
ADAM_EPS = 1e-08
LEARN_RATE = 0.005

NN = ((1,), (0,))
NT = ((1,), (1,))
TN = ((0,), (0,))


def bf16(value):
    return value.astype(jnp.bfloat16)


def f32(value):
    return value.astype(jnp.float32)


def dot(left, right, dims=NN):
    return lax.dot_general(left, right, (dims, ((), ())), preferred_element_type=jnp.float32)


def dot_low(left, right, dims):
    return dot(bf16(left), bf16(right), dims)


def dot_high(left, right, dims):
    left_top, right_top = bf16(left), bf16(right)
    left_rest = bf16(left - f32(left_top))
    right_rest = bf16(right - f32(right_top))
    return (
        dot(left_top, right_top, dims)
        + dot(left_top, right_rest, dims)
        + dot(left_rest, right_top, dims)
    )


def masked_sum(mask, rows, dims):
    top = bf16(rows)
    return dot(mask, top, dims) + dot(mask, bf16(rows - f32(top)), dims)


def gates(forget_raw, lower, keep):
    sigma = jax.nn.sigmoid(forget_raw)
    forget = lower + (1.0 - lower) * sigma
    return sigma, forget, keep * jnp.log(forget), keep * (1.0 - forget)


def causal_mask(rows):
    later = lax.broadcasted_iota(jnp.int32, (rows, rows), 0)
    return later >= lax.broadcasted_iota(jnp.int32, (rows, rows), 1)


def keep_rows(block, rows, length):
    pos = block * rows + lax.broadcasted_iota(jnp.int32, (rows, 1), 0)
    return (pos < length).astype(jnp.float32)


def forward_kernel(count, length, slot, part, core_at, *refs):
    parts, refs = refs[:count], refs[-7:]
    low, gain, core, rec_out, state_out, proj, carry = refs
    step = pl.program_id(0)
    rows, channels = core.shape

    @pl.when(step == 0)
    def _():
        carry[...] = jnp.zeros_like(carry)

    for index in range(count):

        @pl.when(slot[step] == index)
        def _(index=index):
            proj[...] = parts[index][...]

    keep = keep_rows(step, rows, length[0])
    causal = causal_mask(rows)
    ones = causal.astype(jnp.bfloat16)
    for head in range(channels // HEAD):
        cut = pl.ds(head * HEAD, HEAD)
        query_raw = proj[:, cut]
        value = proj[:, pl.ds(2 * channels + head * HEAD, HEAD)]
        lower = low[:, cut]
        forget_raw = proj[:, pl.ds(channels + head * HEAD, HEAD)]
        _, _, logf, key = gates(forget_raw, lower, keep)
        query = query_raw * jax.nn.sigmoid(query_raw)
        run = masked_sum(ones, logf, NN)
        last = run[rows - 1 :, :]
        query_up = query * jnp.exp(run)
        key_down = key * jnp.exp(-run)
        key_tail = key * jnp.exp(last - run)
        state = carry[head]
        state_out[0, head] = state
        scores = jnp.where(causal, dot_low(query_up, key_down, NT), 0.0)
        rec = dot_low(query_up, state, NT) + dot_low(scores, value, NN)
        carry[head] = state * jnp.exp(last) + dot_low(value, key_tail, TN)
        rec_out[:, cut] = rec
        scale = lax.rsqrt(jnp.mean(rec * rec, axis=-1, keepdims=True) + EPS)
        core[:, cut] = bf16(rec * scale * gain[:, cut])


def part_spec(index, wide, last):
    return pl.BlockSpec((CHUNK, wide), lambda i, n, slot, part, *_: (part[index * (last + 1) + i], 0))


def recurrence_forward(length, slot, part, core_at, parts, lower, gain, needed):
    wide = parts[0].shape[1]
    total = len(parts) * parts[0].shape[0]
    channels = wide // 3
    heads = channels // HEAD
    steps = total // CHUNK
    return pl.pallas_call(
        functools.partial(forward_kernel, len(parts)),
        grid_spec=pltpu.PrefetchScalarGridSpec(
            num_scalar_prefetch=4,
            grid=(steps,),
            in_specs=[
                *(part_spec(index, wide, steps - 1) for index in range(len(parts))),
                *(pl.BlockSpec(memory_space=pl.ANY) for _ in needed),
                pl.BlockSpec((1, channels), lambda i, *_: (0, 0)),
                pl.BlockSpec((1, channels), lambda i, *_: (0, 0)),
            ],
            out_specs=[
                pl.BlockSpec((CHUNK, channels), lambda i, n, slot, part, at: (at[i], 0)),
                pl.BlockSpec((CHUNK, channels), lambda i, *_: (i, 0)),
                pl.BlockSpec((1, heads, HEAD, HEAD), lambda i, *_: (i, 0, 0, 0)),
            ],
            scratch_shapes=[
                pltpu.VMEM((CHUNK, wide), jnp.float32),
                pltpu.VMEM((heads, HEAD, HEAD), jnp.float32),
            ],
        ),
        out_shape=[
            jax.ShapeDtypeStruct((total, channels), jnp.bfloat16),
            jax.ShapeDtypeStruct((total, channels), jnp.float32),
            jax.ShapeDtypeStruct((steps, heads, HEAD, HEAD), jnp.float32),
        ],
        compiler_params=pltpu.CompilerParams(vmem_limit_bytes=32 * 1024 * 1024),
        cost_estimate=pl.CostEstimate(
            flops=12 * total * channels * HEAD,
            bytes_accessed=total * channels * 18,
            transcendentals=6 * total * channels,
        ),
        name="recurrence_forward",
    )(length, slot, part, core_at, *parts, *needed, lower, gain)


def backward_kernel(count, length, slot, part, place, slot_core, part_core, *refs):
    parts, gcores, refs = refs[:count], refs[count : 2 * count], refs[-10:]
    low, gain, rec_in, state_in, grad, sums, proj, gcore_in, carry, ends = refs
    step = pl.program_id(0)
    rows, channels = rec_in.shape

    for index in range(count):

        @pl.when(slot[pl.num_programs(0) - 1 - step] == index)
        def _(index=index):
            proj[...] = parts[index][...]

        @pl.when(slot_core[pl.num_programs(0) - 1 - step] == index)
        def _(index=index):
            gcore_in[...] = f32(gcores[index][...])

    @pl.when(step == 0)
    def _():
        carry[...] = jnp.zeros_like(carry)
        ends[...] = jnp.zeros_like(ends)
        sums[...] = jnp.zeros_like(sums)

    keep = keep_rows(pl.num_programs(0) - 1 - step, rows, length[0])
    causal = causal_mask(rows)
    ones = causal.astype(jnp.bfloat16)
    for head in range(channels // HEAD):
        cut = pl.ds(head * HEAD, HEAD)
        cut_forget = pl.ds(channels + head * HEAD, HEAD)
        cut_value = pl.ds(2 * channels + head * HEAD, HEAD)
        query_raw = proj[:, cut]
        value = proj[:, cut_value]
        lower = low[:, cut]
        sigma, forget, logf, key = gates(proj[:, cut_forget], lower, keep)
        sig_query = jax.nn.sigmoid(query_raw)
        query = query_raw * sig_query
        run = masked_sum(ones, logf, NN)
        last = run[rows - 1 :, :]
        up = jnp.exp(run)
        down = jnp.exp(-run)
        tail = jnp.exp(last - run)
        query_up = query * up
        key_down = key * down
        key_tail = key * tail
        rec = rec_in[:, cut]
        gcore = gcore_in[:, cut]
        scale = lax.rsqrt(jnp.mean(rec * rec, axis=-1, keepdims=True) + EPS)
        normed = rec * scale
        weighted = gcore * gain[:, cut]
        grec = scale * (weighted - normed * jnp.mean(normed * weighted, axis=-1, keepdims=True))
        state = state_in[0, head]
        after = carry[head]
        scores = jnp.where(causal, dot_low(query_up, key_down, NT), 0.0)
        gscores = jnp.where(causal, dot_high(grec, value, NT), 0.0)
        gquery_up = dot_high(grec, state, NN) + dot_high(gscores, key_down, NN)
        gkey_down = dot_high(gscores, query_up, TN)
        gkey_tail = dot_high(value, after, NN)
        gvalue = dot_low(scores, grec, TN) + dot_low(key_tail, after, NT)
        carry[head] = after * jnp.exp(last) + dot_low(grec, query_up, TN)
        gquery = gquery_up * up
        gkey = gkey_down * down + gkey_tail * tail
        end = jnp.sum(ends[head] * after, axis=0, keepdims=True)
        ends[head] = state
        glogf = masked_sum(ones, query * gquery - key * gkey, TN) + end
        gforget = keep * (glogf / forget - gkey)
        rising = 1.0 - sigma
        grad[:, cut] = bf16(gquery * sig_query * (1.0 + query_raw * (1.0 - sig_query)))
        grad[:, cut_forget] = bf16(gforget * (1.0 - lower) * sigma * rising)
        grad[:, cut_value] = bf16(gvalue)
        sums[0:1, cut] += jnp.sum(gcore * normed, axis=0, keepdims=True)
        sums[1:2, cut] += jnp.sum(gforget * rising, axis=0, keepdims=True)


def recurrence_backward(length, tables, parts, gcores, lower, gain, rec, states, needed):
    wide = parts[0].shape[1]
    total = len(parts) * parts[0].shape[0]
    channels = wide // 3
    heads = channels // HEAD
    steps = total // CHUNK
    end = steps - 1

    def proj_spec(index):
        return pl.BlockSpec(
            (CHUNK, wide), lambda i, n, slot, part, *_: (part[index * steps + end - i], 0)
        )

    def core_spec(index):
        return pl.BlockSpec(
            (CHUNK, channels),
            lambda i, n, slot, part, place, sc, pc: (pc[index * steps + end - i], 0),
        )

    return pl.pallas_call(
        functools.partial(backward_kernel, len(parts)),
        grid_spec=pltpu.PrefetchScalarGridSpec(
            num_scalar_prefetch=6,
            grid=(steps,),
            in_specs=[
                *(proj_spec(index) for index in range(len(parts))),
                *(core_spec(index) for index in range(len(parts))),
                *(pl.BlockSpec(memory_space=pl.ANY) for _ in needed),
                pl.BlockSpec((1, channels), lambda i, *_: (0, 0)),
                pl.BlockSpec((1, channels), lambda i, *_: (0, 0)),
                pl.BlockSpec((CHUNK, channels), lambda i, *_: (end - i, 0)),
                pl.BlockSpec((1, heads, HEAD, HEAD), lambda i, *_: (end - i, 0, 0, 0)),
            ],
            out_specs=[
                pl.BlockSpec((CHUNK, wide), lambda i, n, slot, part, place, *_: (place[end - i], 0)),
                pl.BlockSpec((8, channels), lambda i, *_: (0, 0)),
            ],
            scratch_shapes=[
                pltpu.VMEM((CHUNK, wide), jnp.float32),
                pltpu.VMEM((CHUNK, channels), jnp.float32),
                pltpu.VMEM((heads, HEAD, HEAD), jnp.float32),
                pltpu.VMEM((heads, HEAD, HEAD), jnp.float32),
            ],
        ),
        out_shape=[
            jax.ShapeDtypeStruct((total, wide), jnp.bfloat16),
            jax.ShapeDtypeStruct((8, channels), jnp.float32),
        ],
        compiler_params=pltpu.CompilerParams(vmem_limit_bytes=32 * 1024 * 1024),
        cost_estimate=pl.CostEstimate(
            flops=40 * total * channels * HEAD,
            bytes_accessed=total * channels * 26,
            transcendentals=8 * total * channels,
        ),
        name="recurrence_backward",
    )(length, *tables, *parts, *gcores, *needed, lower, gain, rec, states)


class Ring:
    def __init__(self, axis):
        size = lax.axis_size(axis)
        ring = [0, *range(1, size, 2), *range(size - 2, 0, -2)]
        self.axis, self.size = axis, size
        self.ahead = [(ring[i], ring[(i + 1) % size]) for i in range(size)]
        self.owner_of_slot = np.zeros((size, size), np.int32)
        for at, me in enumerate(ring):
            self.owner_of_slot[me] = [ring[at - slot] for slot in range(size)]

    def send(self, value):
        return lax.ppermute(value, self.axis, self.ahead)

    def gather(self, own, held=lambda slots: ()):
        slots = [own]
        for _ in range(1, self.size):
            got = self.send(slots[-1])
            slots.append(after(got, *held(slots)))
        return slots

    def scatter(self, parts):
        total = self.send(parts[1])
        for step in range(2, self.size):
            needed = (yield total) or ()
            total = self.send(bf16(f32(after(parts[step], *needed)) + f32(total)))
        needed = (yield total) or ()
        yield f32(after(parts[0], *needed)) + f32(total)


def flip(value, axis, bit):
    return lax.ppermute(value, axis, [(i, i ^ (1 << bit)) for i in range(lax.axis_size(axis))])


class Halving:
    def __init__(self, value, axis, order):
        size = lax.axis_size(axis)
        bits = size.bit_length() - 1
        self.axis, self.order, self.left = axis, list(order), list(range(bits - 1, -1, -1))
        self.value = value.reshape((2,) * bits + (value.shape[0] // size, value.shape[1]))

    def step(self, *needed):
        bit = self.order.pop(0)
        at, mine = self.left.index(bit), (lax.axis_index(self.axis) >> bit) & 1
        sent = lax.dynamic_index_in_dim(self.value, 1 - mine, at, keepdims=False)
        kept = lax.dynamic_index_in_dim(self.value, mine, at, keepdims=False)
        got = flip(after(sent, *needed), self.axis, bit)
        self.left.pop(at)
        total = f32(kept) + f32(got)
        self.value = bf16(total) if self.order else total
        return got


class HalvingColumns:
    def __init__(self, value, axis, order):
        self.axis, self.order, self.value = axis, list(order), value

    def step(self, *needed):
        bit, half = self.order.pop(0), self.value.shape[1] // 2
        got = flip(after(self.value[:, half:], *needed), self.axis, bit)
        total = f32(self.value[:, :half]) + f32(got)
        self.value = bf16(total) if self.order else total
        return got


def doubled(value, axis, order):
    known = []
    for bit in order:
        got = flip(value, axis, bit)
        mine = ((lax.axis_index(axis) >> bit) & 1) == 1
        at = sum(other > bit for other in known)
        value = jnp.stack([jnp.where(mine, got, value), jnp.where(mine, value, got)], at)
        known.append(bit)
        needed = yield value
        value = after(value, *(needed or ()))


def after(value, *needed):
    return lax.optimization_barrier((value, needed))[0] if needed else value


def behind(value, mark):
    return jnp.where(mark > 3.0e38, mark, value)


def permute_kernel(blocks, order, value, out):
    block = value.shape[1] // blocks
    for i in range(blocks):
        cut = pl.ds(pl.multiple_of(order[i] * block, block), block)
        out[:, pl.ds(i * block, block)] = value[:, cut]


def permute_columns(value, order):
    blocks = order.shape[0]
    whole = pl.BlockSpec(value.shape, lambda i, *_: (0, 0))
    return pl.pallas_call(
        functools.partial(permute_kernel, blocks),
        grid_spec=pltpu.PrefetchScalarGridSpec(
            num_scalar_prefetch=1, grid=(1,), in_specs=[whole], out_specs=whole
        ),
        out_shape=jax.ShapeDtypeStruct(value.shape, value.dtype),
        name="permute_columns",
    )(order, value)


def column_order(axis, order):
    size, me = lax.axis_size(axis), lax.axis_index(axis)
    bits = size.bit_length() - 1
    offsets = [
        sum(((at >> (bits - 1 - i)) & 1) << bit for i, bit in enumerate(order)) for at in range(size)
    ]
    return jnp.asarray(np.array(offsets, np.int32)) ^ me.astype(jnp.int32)


def bit_orders(axis):
    upper = list(range(1, lax.axis_size(axis).bit_length() - 1))
    return [0, *upper], [0, *upper[::-1]]


def sum_all(value, axes):
    for axis in axes:
        for bit in range(lax.axis_size(axis).bit_length() - 1):
            value = value + flip(value, axis, bit)
    return value


def copy_kernel(value, out):
    out[...] = value[...]


def copied(value):
    outer, rows, width = value.shape
    spec = pl.BlockSpec((1, rows // 4, width), lambda i, j: (i, j, 0))
    return pl.pallas_call(
        copy_kernel,
        grid=(outer, 4),
        in_specs=[spec],
        out_specs=spec,
        out_shape=jax.ShapeDtypeStruct(value.shape, value.dtype),
        name="copied",
    )(value)


def by_slot(value, size):
    rows = value.shape[0] // size
    return [value[slot * rows : (slot + 1) * rows] for slot in range(size)]


def norm_back(value, scale, gain, grad):
    inner = jnp.mean(value * gain * grad, axis=-1, keepdims=True)
    return scale * gain * grad - value * (scale * scale * scale) * inner


def inverse_rms(value):
    return lax.rsqrt(jnp.mean(value * value, axis=-1, keepdims=True) + EPS)


def moments(first, second, grad):
    first = BETA_ONE * first + (1.0 - BETA_ONE) * grad
    second = BETA_TWO * second + (1.0 - BETA_TWO) * grad * grad
    return (first, second)


def adamw(param, first, second, grad):
    first, second = moments(first, second, grad)
    fix_one = 1.0 - BETA_ONE**STEP
    fix_two = 1.0 - BETA_TWO**STEP
    update = first / fix_one / (jnp.sqrt(second / fix_two) + ADAM_EPS) + DECAY * param
    return (param - LEARN_RATE * update, first, second)


def body(
    block_input,
    cotangent,
    lengths,
    vectors,
    vectors_first,
    vectors_second,
    mixer_in,
    mixer_in_first,
    mixer_in_second,
    mixer_out,
    mixer_out_first,
    mixer_out_second,
    ffn_in,
    ffn_in_first,
    ffn_in_second,
    ffn_out,
    ffn_out_first,
    ffn_out_second,
):
    own_rows, width = block_input.shape
    group = lax.axis_index("dp")
    member = lax.axis_index("mp")
    members = lax.axis_size("mp")
    ring = Ring("mp")
    length = lax.dynamic_index_in_dim(lengths, group, 0, keepdims=True)
    own_pos = member * own_rows + jnp.arange(own_rows, dtype=jnp.int32)
    keep = f32(own_pos < length[0])[:, None]
    channels = mixer_in.shape[2]
    channel_start = member * channels
    group_gain = lax.dynamic_slice_in_dim(vectors[1:2], channel_start, channels, 1)
    lower = lax.dynamic_slice_in_dim(vectors[2:3], channel_start, channels, 1)

    per = own_rows // CHUNK
    blocks = jnp.arange(members * per, dtype=jnp.int32)
    owner_of_slot = jnp.asarray(ring.owner_of_slot)[member]
    slot = jnp.asarray(np.argsort(ring.owner_of_slot, 1).astype(np.int32))[member][blocks // per]
    part = jnp.clip(blocks[None, :] - owner_of_slot[:, None] * per, 0, per - 1).reshape(-1)
    place = slot * per + blocks % per

    in_shard = jnp.concatenate([bf16(mixer_in[j]) for j in range(3)], 1)
    half_in = 3 * channels // 2
    halves_in = (slice(0, half_in), slice(half_in, None))
    order_one, order_two = bit_orders("dp")
    inputs = f32(block_input)
    scale_one = inverse_rms(inputs)
    own_one = bf16(inputs * scale_one * vectors[0])
    weight_in = lax.all_gather(in_shard, "dp", axis=0, tiled=True)
    order_out = column_order("dp", order_one)
    weight_out = lax.all_gather(bf16(mixer_out), "dp", axis=1, tiled=True)
    weight_gate_up = lax.all_gather(bf16(ffn_in), "dp", axis=1, tiled=True)
    weight_down = lax.all_gather(bf16(ffn_out), "dp", axis=1, tiled=True)
    proj = []

    def project(slots):
        if len(slots) > 2:
            proj.append(dot(slots[len(proj)], weight_in))
        return proj[-1:]

    normed_one = ring.gather(own_one, project)
    while len(proj) < members:
        project(normed_one)

    grad_total = f32(cotangent) * keep
    grad_rows = ring.gather(after(bf16(grad_total), normed_one[-1]))
    core, rec, states = recurrence_forward(length, slot, part, place, proj, lower, group_gain, ())
    mix_parts = by_slot(bf16(dot(core, weight_out)), members)
    mix_parts[1] = after(mix_parts[1], grad_rows[1])
    steps = ring.scatter(mix_parts)
    for _ in range(members - 1):
        next(steps)
    mix = next(steps)
    resid = inputs + mix
    scale_two = inverse_rms(resid)

    hidden, grad_gate, grad_up, two_parts = [], [], [], []

    def feed(slots):
        rows, grows = slots[-1], grad_rows[len(slots) - 1]
        gate, up = dot(rows, weight_gate_up[0]), dot(rows, weight_gate_up[1])
        sigma = jax.nn.sigmoid(gate)
        act = gate * sigma
        hidden.append(bf16(act * up))
        ghid = dot(grows, weight_down, NT)
        grad_gate.append(bf16(ghid * up * sigma * (1.0 + gate * (1.0 - sigma))))
        grad_up.append(bf16(ghid * act))
        two_parts.append(
            bf16(
                dot(grad_gate[-1], weight_gate_up[0], NT) + dot(grad_up[-1], weight_gate_up[1], NT)
            )
        )
        return two_parts[-1:]

    normed_two = ring.gather(bf16(resid * scale_two * vectors[3]), feed)
    steps = ring.scatter(two_parts)
    normed_two[-1] = after(normed_two[-1], next(steps))
    feed(normed_two)
    for _ in range(members - 4):
        steps.send(())
    came = steps.send(())
    normed_two_all = jnp.concatenate(normed_two, 0)
    sum_gate_up = jnp.stack(
        [
            bf16(dot(normed_two_all, after(jnp.concatenate(part, 0), *two_parts), TN))
            for part in (grad_gate, grad_up)
        ]
    )
    shard_gate_up = lax.psum_scatter(sum_gate_up, "dp", scatter_dimension=1, tiled=True)
    hidden_all = after(jnp.concatenate(hidden, 0), came)
    sum_down = bf16(dot(hidden_all, jnp.concatenate(grad_rows, 0), TN))
    shard_down = lax.psum_scatter(sum_down, "dp", scatter_dimension=1, tiled=True)
    ffn_parts = by_slot(bf16(dot(hidden_all, weight_down)), members)
    steps.send(())
    grad_two = steps.send((sum_gate_up,))

    grad_resid = grad_total + norm_back(resid, scale_two, vectors[3], grad_two)
    gain_two = jnp.sum(grad_two * resid * scale_two, axis=0)

    weight_out = permute_columns(weight_out, order_out)
    grad_core = []

    def pull(slots):
        grad_core.append(bf16(dot(slots[-1], weight_out, NT)))
        return [*grad_core[-1:], *ffn_parts[: len(slots) // 2]]

    grad_mix = ring.gather(permute_columns(bf16(grad_resid), order_out), pull)
    grad_core.append(bf16(dot(grad_mix[-1], weight_out, NT)))
    grad_proj, sums = recurrence_backward(
        length,
        (slot, part, place, slot, part),
        proj,
        grad_core,
        lower,
        group_gain,
        rec,
        states,
        (),
    )
    mark = sums[0, 0]
    ffn_parts[1] = after(ffn_parts[1], grad_mix[-1])
    ffn_parts[2] = behind(ffn_parts[2], bf16(mark))
    steps = ring.scatter(ffn_parts)
    one = next(steps)
    sum_out = bf16(dot(behind(core, bf16(mark)), jnp.concatenate(grad_mix, 0), TN))
    out_sum = HalvingColumns(sum_out, "dp", order_one)
    shard_gate_up = behind(f32(shard_gate_up), mark)
    gu_new, gu_first, gu_second = adamw(ffn_in, ffn_in_first, ffn_in_second, shard_gate_up)
    gu_sent = bf16(gu_new)
    done = [out_sum.step()]

    two = steps.send((grad_proj, *done))
    grad_proj = after(grad_proj, one)
    normed_one_all = jnp.concatenate(normed_one, 0)
    sum_in = [bf16(dot(normed_one_all, grad_proj[:, cut], TN)) for cut in halves_in]
    in_sums = [Halving(piece, "dp", order) for piece, order in zip(sum_in, (order_one, order_two))]
    done = [out_sum.step(one), *(item.step() for item in in_sums)]

    shard_down = behind(f32(shard_down), f32(sum_in[0][0, 0]))
    down_new, down_first, down_second = adamw(ffn_out, ffn_out_first, ffn_out_second, shard_down)
    down_sent = bf16(down_new)

    three = steps.send((*sum_in, gu_sent))
    grad_proj = after(grad_proj, two)
    one_parts = by_slot(bf16(dot(grad_proj, weight_in, NT)), members)
    done += [item.step(two) for item in in_sums]
    while out_sum.order:
        done.append(out_sum.step(two))
    for _ in range(members - 4):
        three = steps.send(())
    ffn = steps.send((*one_parts, *done, down_sent))
    total = resid + ffn
    one_parts[1] = after(one_parts[1], ffn)

    steps = ring.scatter(one_parts)
    one = next(steps)
    while in_sums[0].order:
        done = [item.step(three) for item in in_sums]
    shard_out = after(out_sum.value, three)
    out_new, out_first, out_second = adamw(mixer_out, mixer_out_first, mixer_out_second, shard_out)
    out_sent = bf16(out_new)
    gain_one = sum(
        jnp.sum(f32(weight_in[:, cut]) * f32(piece), axis=1)
        for cut, piece in zip(halves_in, after(sum_in, three))
    )
    blank = jnp.zeros((width,), jnp.float32)
    squares = jnp.stack([jnp.sum(keep * piece * piece) for piece in (total, mix, ffn)])
    vector_part = jnp.stack(
        [
            gain_one / vectors[0],
            lax.dynamic_update_slice_in_dim(blank, sums[0], channel_start, 0),
            lax.dynamic_update_slice_in_dim(blank, sums[1], channel_start, 0),
            gain_two,
            lax.dynamic_update_slice_in_dim(blank, squares, 0, 0),
        ]
    )


    two = steps.send((vector_part, out_sent, *done))
    shard_in = jnp.concatenate([after(item.value, one) for item in in_sums], 1)
    shard_in = jnp.stack([shard_in[:, j * channels : (j + 1) * channels] for j in range(3)])
    in_new, in_first, in_second = adamw(mixer_in, mixer_in_first, mixer_in_second, shard_in)
    in_sent = bf16(in_new)
    half = channels // 2
    spread = [
        doubled(piece, "dp", order[::-1])
        for piece, order in zip((in_sent[:, :, :half], in_sent[:, :, half:]), (order_one, order_two))
    ]
    for _ in order_one[1:]:
        in_low = [next(piece) for piece in spread]
    vector_sums = sum_all(behind(vector_part, f32(two[0, 0])), ("dp",))

    gu_low = copied(lax.all_gather(gu_sent, "dp", axis=1, tiled=True))
    one_parts[-1] = behind(one_parts[-1], gu_low[0, 0, 0])
    three = steps.send(in_low)
    for _ in range(members - 4):
        three = steps.send(())
    grad_one = steps.send(())
    vector_sums = sum_all(after(vector_sums, three), ("mp",))
    in_low = jnp.concatenate([next(piece) for piece in spread], -1)
    in_low = jnp.moveaxis(in_low, len(order_one), 0).reshape(3, width, channels)
    input_grad = grad_resid + norm_back(inputs, scale_one, vectors[0], grad_one)
    vectors_grad = vector_sums[:4]
    denom = f32(jnp.sum(lengths)) * width
    stats = jnp.sqrt(vector_sums[4, :3] / denom)
    vec_first, vec_second = moments(vectors_first, vectors_second, vectors_grad)

    down_low, out_low = (
        lax.all_gather(new, "dp", axis=1, tiled=True) for new in (down_sent, out_sent)
    )
    return (
        bf16(total),
        input_grad,
        stats,
        vectors_grad,
        vec_first,
        vec_second,
        shard_in,
        in_new,
        in_first,
        in_second,
        in_low,
        shard_out,
        out_new,
        out_first,
        out_second,
        out_low,
        shard_gate_up,
        gu_new,
        gu_first,
        gu_second,
        gu_low,
        shard_down,
        down_new,
        down_first,
        down_second,
        down_low,
    )


def solution(mesh):
    rows = P(("dp", "mp"), None)
    deep = P(None, "dp", "mp")
    flat = P("mp", "dp")
    in_specs = (
        (rows, rows, P(), P(), P(), P()) + (deep,) * 3 + (flat,) * 3 + (deep,) * 3 + (flat,) * 3
    )
    wide = (deep,) * 4 + (P(None, None, "mp"),)
    tall = (flat,) * 4 + (P("mp", None),)
    out_specs = (rows, rows, P(), P(), P(), P()) + wide + tall + wide + tall
    return jax.shard_map(body, mesh=mesh, in_specs=in_specs, out_specs=out_specs, check_vma=False)
```
